512 devices in a mesh: grp: 32 (over x, y, core), blk: 16 (over z).
Axes of the slice: x: 4, y: 4, z: 16, core: 2. Of those that a mesh axis runs over, the one named last changes fastest.
Arguments:
- dual_populace: float32 [19, 256, 256, 128], P(None, 'grp', 'blk'), may hold values from -6 to 6
- forward_motion_vector: float32 [3, 256, 256, 128], P(None, 'grp', 'blk'), may hold values from -0.4 to 0.4
- forward_heat_level: float32 [256, 256, 128], P('grp', 'blk'), may hold values from 0.5 to 1.5
- objective_heat_gradient: float32 [256, 256, 128], P('grp', 'blk'), may hold values from -6 to 6
- liquid_indicator: int32 [256, 256, 128], P('grp', 'blk'), may hold values 0 or 1
- filter_span_group: int32 [256, 256, 128], P('grp', 'blk'), may hold values from 0 to 3
Outputs:
- adjoint_out: float32 [19, 256, 256, 128], P(None, 'grp', 'blk')
- filtered: float32 [256, 256, 128], P('grp', 'blk')
The draws below stay inside these ranges and needn't reach their ends.
All inputs are finite; a program needn't handle non-finite values. No bound on the sum of `liquid_indicator` on one device may be relied on, other than what follows from the above.
Results may differ from the reference program's by a relative error of at most 0.000031.
Values sent between devices are 32-bit elements; how exact they have to be, the bound alone decides.
A program may use at most 64 MiB of HBM per device.

```python
import jax
import jax.numpy as jnp

POPS = 19
STEPS = 3
SWEEPS = 8
NODES_LEADING = 256
NODES_MIDDLING = 256
NODES_TRAILING = 128


def set_ends(array, rng, smallest, top_value):
    index_at = [jax.random.randint(jax.random.fold_in(rng, axis), (), 0, length) for axis, length in enumerate(array.shape)]
    main_axis = array.shape.index(max(array.shape))
    beside = index_at[:main_axis] + [(index_at[main_axis] + 1) % array.shape[main_axis]] + index_at[main_axis + 1:]
    return array.at[tuple(index_at)].set(smallest).at[tuple(beside)].set(top_value)


def steps_of(key, extent, split, least, high):
    loudness, own = 1.0, jax.random.fold_in(key, 6)
    for dim, parts in split:
        heights = jnp.exp(jax.random.uniform(jax.random.fold_in(own, dim), (parts,), jnp.float32, least / len(split), high / len(split)))
        loudness = loudness * jnp.repeat(heights, extent[dim] // parts).reshape([-1 if axis == dim else 1 for axis in range(len(extent))])
    return loudness


def normal_values(stream_key, extent, spread, reach, cuts=(), kind=jnp.bfloat16):
    result = jax.random.normal(stream_key, extent, jnp.float32) * spread
    if len(cuts) > 0:
        result = steps_of(stream_key, extent, cuts, -0.22, 0.18) * result
    return jnp.clip(result, min=-reach, max=reach).astype(kind)


def setup_inputs(seed: int = 0) -> dict:
    splits = jax.random.split(jax.random.key(seed), 7)
    return {
        "dual_populace": normal_values(splits[0], (POPS, NODES_LEADING, NODES_MIDDLING, NODES_TRAILING), 1.0, 6.0, ((1, 32), (2, 16)), jnp.float32),
        "forward_motion_vector": normal_values(splits[1], (3, NODES_LEADING, NODES_MIDDLING, NODES_TRAILING), 0.1, 0.4, ((1, 32), (2, 16)), jnp.float32),
        "forward_heat_level": jnp.clip(0.5 + 1.0 * jax.random.uniform(splits[2], (NODES_LEADING, NODES_MIDDLING, NODES_TRAILING), jnp.float32) ** steps_of(splits[2], (NODES_LEADING, NODES_MIDDLING, NODES_TRAILING), ((0, 32), (1, 16)), -0.2, 0.2), 0.5, 1.5),
        "objective_heat_gradient": normal_values(splits[3], (NODES_LEADING, NODES_MIDDLING, NODES_TRAILING), 1.0, 6.0, ((0, 32), (1, 16)), jnp.float32),
        "liquid_indicator": set_ends((jax.random.randint(splits[4], (NODES_LEADING, NODES_MIDDLING, NODES_TRAILING), 0, 4) < 3).astype(jnp.int32), jax.random.fold_in(splits[4], 1), 0, 1),
        "filter_span_group": set_ends(jax.random.randint(splits[5], (NODES_LEADING, NODES_MIDDLING, NODES_TRAILING), 0, 4), jax.random.fold_in(splits[5], 1), 0, 3).astype(jnp.int32),
    }


VELOCITIES = ((0, 0, 0), (1, 0, 0), (-1, 0, 0), (0, 1, 0), (0, -1, 0), (0, 0, 1), (0, 0, -1),
              (1, 1, 0), (-1, -1, 0), (1, -1, 0), (-1, 1, 0), (1, 0, 1), (-1, 0, -1), (1, 0, -1),
              (-1, 0, 1), (0, 1, 1), (0, -1, -1), (0, 1, -1), (0, -1, 1))
WEIGHTS = (1.0 / 3.0,) + (1.0 / 18.0,) * 6 + (1.0 / 36.0,) * 12


def collide(pulled, omega, vel_x, vel_y, vel_z, objective_heat_gradient):
    equilib = jnp.zeros_like(omega)
    average = jnp.zeros_like(omega)
    for population in range(19):
        cx, cy, cz = VELOCITIES[population]
        along = cx * vel_x + cy * vel_y + cz * vel_z
        equilib = equilib + WEIGHTS[population] * (1.0 + 3.0 * along) * pulled[population]
        average = average + WEIGHTS[population] * pulled[population]
    posts = [pulled[population] - omega * (pulled[population] - equilib) + WEIGHTS[population] * objective_heat_gradient
             for population in range(19)]
    return jnp.stack(posts), equilib - average


def pull_all(state):
    width_x, width_y, width_z = state.shape[1], state.shape[2], state.shape[3]
    padded = jnp.pad(state, ((0, 0), (1, 1), (1, 1), (1, 1)))
    pieces = []
    for population in range(19):
        cx, cy, cz = VELOCITIES[population]
        pieces.append(padded[population, 1 + cx:1 + cx + width_x, 1 + cy:1 + cy + width_y, 1 + cz:1 + cz + width_z])
    return jnp.stack(pieces)


def reference(dual_populace, forward_motion_vector, forward_heat_level, objective_heat_gradient, liquid_indicator, filter_span_group):
    fluid = liquid_indicator.astype(jnp.float32)
    moving = forward_motion_vector * fluid[None]
    omega = 0.9 + 0.7 * fluid
    state = dual_populace
    gradient_map = jnp.zeros_like(forward_heat_level)
    for number in range(STEPS):
        pulled = pull_all(state)
        state, correction_increment = collide(pulled, omega, moving[0], moving[1], moving[2], objective_heat_gradient)
        gradient_map = gradient_map + forward_heat_level * correction_increment
    radius_sq = 0.25 * jnp.power(4.0, filter_span_group.astype(jnp.float32))
    denom = 1.0 + 6.0 * radius_sq
    smooth = gradient_map
    for number in range(SWEEPS):
        padded = jnp.pad(smooth, 1)
        beside = padded[2:, 1:-1, 1:-1] + padded[:-2, 1:-1, 1:-1]
        beside = beside + padded[1:-1, 2:, 1:-1] + padded[1:-1, :-2, 1:-1]
        beside = beside + padded[1:-1, 1:-1, 2:] + padded[1:-1, 1:-1, :-2]
        smooth = (gradient_map + radius_sq * beside) / denom
    return state, smooth
```

```python
import math

import jax
import jax.numpy as jnp
from jax import lax
from jax.experimental import pallas as pl
from jax.experimental.pallas import tpu as pltpu
from jax.sharding import PartitionSpec as P

MESH = pl.DeviceIdType.MESH
SWEEPS = 8
VELOCITIES = (
    (0, 0, 0),
    (1, 0, 0),
    (-1, 0, 0),
    (0, 1, 0),
    (0, -1, 0),
    (0, 0, 1),
    (0, 0, -1),
    (1, 1, 0),
    (-1, -1, 0),
    (1, -1, 0),
    (-1, 1, 0),
    (1, 0, 1),
    (-1, 0, -1),
    (1, 0, -1),
    (-1, 0, 1),
    (0, 1, 1),
    (0, -1, -1),
    (0, 1, -1),
    (0, -1, 1),
)
DIRS = ((1, 0), (-1, 0), (0, 1), (0, -1), (1, 1), (1, -1), (-1, 1), (-1, -1))
NX, NY, NZ = 8, 16, 128
X0, XF, Y0 = 3, 8, 16
ROWS = 48
STEP_X, FILTER_X = NX + 2 * X0, NX + 2 * XF
def src_span(side, length, first, last):
    if side > 0:
        return pl.ds(length - last, last - first + 1)
    if side < 0:
        return pl.ds(first - 1, last - first + 1)
    return pl.ds(0, length)


def dst_span(side, length, own, first, last):
    if side > 0:
        return pl.ds(own - last, last - first + 1)
    if side < 0:
        return pl.ds(own + length + first - 1, last - first + 1)
    return pl.ds(own, length)


def planes(first, end, together, body):
    main = (end - first) // together * together

    if main > together:

        @pl.loop(first, first + main, step=together)
        def _(x):
            for j in range(together):
                body(x + j)

    else:
        main = 0
    for x in range(first + main, end):
        body(x)


def runs_of(sx, sy):
    runs = []
    for i, (cx, cy, _) in enumerate(VELOCITIES):
        depth = (2 - sx * cx, 2 - sy * cy)
        if runs and runs[-1][2] == depth:
            runs[-1] = (runs[-1][0], runs[-1][1] + 1, depth)
        else:
            runs.append((i, 1, depth))
    return runs


def rows_in(*parts):
    return sum(math.prod(p.shape) // NZ for p in parts)


def exchange_kernel(
    pop, vel, heat, obj, liq, span,
    state_out, sens, scale_out, gain_out,
    s0, s1, u0, obj0, liq0, span0, heat0, um, ka, kb, dsum, count,
    load_sem, ssem, rsem, ready,
):
    grp, blk = lax.axis_index("grp"), lax.axis_index("blk")
    n_grp, n_blk = lax.axis_size("grp"), lax.axis_size("blk")
    late = (grp == 0) & (blk == 0)

    def exists(d):
        ok = None
        for side, at, n in ((d[0], grp, n_grp), (d[1], blk, n_blk)):
            if side:
                one = at < n - 1 if side > 0 else at > 0
                ok = one if ok is None else ok & one
        return ok

    def to_late(d):
        return (grp + d[0] == 0) & (blk + d[1] == 0)

    def opposite(d):
        return (-d[0], -d[1])

    def peer(d):
        return dict(device_id=(grp + d[0], blk + d[1]), device_id_type=MESH)

    def remote(d, j, src, dst):
        k = DIRS.index(d)
        return pltpu.make_async_remote_copy(
            src_ref=src, dst_ref=dst, send_sem=ssem.at[j, k], recv_sem=rsem.at[j, k], **peer(d)
        )

    def part(d, src, dst, lead, depth, own_x):
        xs, ys = src_span(d[0], NX, 1, depth[0]), src_span(d[1], NY, 1, depth[1])
        xd = dst_span(d[0], NX, own_x, 1, depth[0])
        yd = dst_span(d[1], NY, Y0, 1, depth[1])
        return src.at[lead + (xs, ys)], dst.at[lead + (xd, yd)]

    def state_parts(d):
        parts = [part(d, pop, s0, (pl.ds(a, n),), depth, X0) for a, n, depth in runs_of(*d)]
        parts.append(part(d, vel, u0, (pl.ds(0, 3),), (2, 2), X0))
        parts.append(part(d, obj, obj0, (), (2, 2), X0))
        parts.append(part(d, liq, liq0, (), (2, 2), X0))
        return parts

    def filter_pieces(d):
        dx, dy = d
        if dx and dy:
            near = ((1, 3, 1, 7), (4, 7, 1, 4))
        else:
            near = ((1, XF, 1, XF),)
        return [
            (src_span(dx, NX, a, b), src_span(dy, NY, c, e),
             dst_span(dx, NX, XF, a, b), dst_span(dy, NY, Y0, c, e))
            for a, b, c, e in near
        ]

    def span_parts(d):
        return [(span.at[xs, ys], span0.at[xd, yd]) for xs, ys, xd, yd in filter_pieces(d)]

    def sens_parts(d):
        return [
            (sens.at[pl.ds(xs.start + XF, xs.size), pl.ds(ys.start + Y0, ys.size)], sens.at[xd, yd])
            for xs, ys, xd, yd in filter_pieces(d)
        ]

    stages = (state_parts, span_parts, sens_parts)

    def send(j, d):
        for src, dst in stages[j](d):
            remote(d, j, src, dst).start()

    def whole(j, d):
        rows = count.at[pl.ds(0, rows_in(*(src for src, _ in stages[j](d))))]
        return remote(d, j, rows, rows)

    def wait_recv(j):
        for d in DIRS:
            pl.when(exists(opposite(d)))(lambda d=d: whole(j, d).wait_recv())

    barrier = pltpu.get_barrier_semaphore()
    expected = 0
    for d in DIRS:
        pl.when(exists(d) & ~late)(lambda d=d: pl.semaphore_signal(barrier, inc=1, **peer(d)))
        expected += jnp.where(exists(d) & ~to_late(d), 1, 0)
    pl.semaphore_wait(barrier, expected)

    @pl.when(late)
    def _():
        for d in ((0, 1), (1, 1), (1, 0)):
            pl.semaphore_signal(ready, inc=1, **peer(d))

    order = ((0, 1), (0, -1), (1, 0), (-1, 0), (1, 1), (1, -1), (-1, 1), (-1, -1))
    for d in order:
        pl.when(exists(d) & ~to_late(d))(lambda d=d: send(0, d))

    own = (pl.ds(X0, NX), pl.ds(Y0, NY))
    loads = [
        pltpu.make_async_copy(src, dst, load_sem.at[j])
        for j, (src, dst) in enumerate(
            (
                (pop, s0.at[(pl.ds(0, 19),) + own]),
                (vel, u0.at[(pl.ds(0, 3),) + own]),
                (obj, obj0.at[own]),
                (liq, liq0.at[own]),
                (heat, heat0),
                (span, span0.at[pl.ds(XF, NX), pl.ds(Y0, NY)]),
            )
        )
    ]
    for c in loads:
        c.start()
    for d in order:
        pl.when(exists(d) & ~to_late(d))(lambda d=d: send(1, d))

    def outside(x_step, x_filter, rows):
        def fill(first, count, width, put):
            @pl.loop(first, first + count)
            def _(x):
                for r in rows:
                    put(x, pl.ds(r, 8))

        zero = jnp.zeros((8, NZ), jnp.float32)
        none = jnp.full((8, NZ), -1, jnp.int32)

        def put_step(x, r):
            for i in range(19):
                s0[i, x, r] = zero
            for i in range(3):
                u0[i, x, r] = zero
            obj0[x, r] = zero
            liq0[x, r] = none

        def put_filter(x, r):
            span0[x, r] = none
            sens[x, r] = zero

        fill(*x_step, None, put_step)
        fill(*x_filter, None, put_filter)

    groups = (8, 16, 24, 32)
    pl.when(grp == 0)(lambda: outside((0, X0), (0, XF), groups))
    pl.when(grp == n_grp - 1)(lambda: outside((X0 + NX, X0), (XF + NX, XF), groups))
    pl.when(blk == 0)(lambda: outside((0, STEP_X), (0, FILTER_X), (8,)))
    pl.when(blk == n_blk - 1)(lambda: outside((0, STEP_X), (0, FILTER_X), (32,)))

    for d in ((0, -1), (-1, -1), (-1, 0)):

        @pl.when(exists(d) & to_late(d))
        def _():
            pl.semaphore_wait(ready, 1)
            send(0, d)
            send(1, d)

    for c in loads:
        c.wait()
    wait_recv(0)

    lane = lax.broadcasted_iota(jnp.int32, (8, NZ), 1)

    def step(number, src, x, r0):
        def pulled(i):
            cx, cy, cz = VELOCITIES[i]
            v = src[i, x + cx, pl.ds(r0 + cy, 8)]
            if cz > 0:
                return jnp.where(lane == NZ - 1, 0.0, pltpu.roll(v, NZ - 1, 1))
            if cz < 0:
                return jnp.where(lane == 0, 0.0, pltpu.roll(v, 1, 1))
            return v

        p = [pulled(i) for i in range(19)]
        rows = pl.ds(r0, 8)
        if number == 0:
            kind = liq0[x, rows]
            fluid = kind.astype(jnp.float32)
            inside = kind >= 0
            omega = 0.9 + 0.7 * fluid
            b = jnp.where(inside, omega, 0.0)
            a = jnp.where(inside, 1.0 - omega, 0.0)
            third = fluid * (3.0 / 36.0)
            ux, uy, uz = (u0[i, x, rows] * third for i in range(3))
            ka[x, rows] = a
            kb[x, rows] = b
            um[0, x, rows] = ux
            um[1, x, rows] = uy
            um[2, x, rows] = uz
        else:
            a, b = ka[x, rows], kb[x, rows]
            ux, uy, uz = (um[i, x, rows] for i in range(3))
        total = {i: p[i] + p[i + 1] for i in range(1, 19, 2)}
        diff = {i: p[i] - p[i + 1] for i in range(1, 19, 2)}
        faces = total[1] + total[3] + total[5]
        edges = (total[7] + total[9]) + (total[11] + total[13]) + (total[15] + total[17])
        average = p[0] * (1.0 / 3.0) + faces * (1.0 / 18.0) + edges * (1.0 / 36.0)
        mx = (diff[1] + diff[1]) + (diff[7] + diff[9]) + (diff[11] + diff[13])
        my = (diff[3] + diff[3]) + (diff[7] - diff[9]) + (diff[15] + diff[17])
        mz = (diff[5] + diff[5]) + (diff[11] - diff[13]) + (diff[15] - diff[17])
        extra = ux * mx + uy * my + uz * mz
        pushed = b * (average + extra)
        o = obj0[x, rows] * (1.0 / 36.0)
        o2 = o + o
        adds = (pushed + 12.0 * o, pushed + o2, pushed + o)
        return [a * p[i] + adds[0 if i == 0 else 1 if i < 7 else 2] for i in range(19)], extra

    def step_1(x):
        for r0 in groups:
            posts, extra = step(0, s0, x, r0)
            for i in range(19):
                s1[i, x, pl.ds(r0, 8)] = posts[i]
            if r0 in (16, 24):
                dsum[x, pl.ds(r0, 8)] = extra

    planes(1, STEP_X - 1, 2, step_1)

    def step_2(x):
        for r0 in groups:
            posts, extra = step(1, s1, x, r0)
            for i in range(19):
                s0[i, x, pl.ds(r0, 8)] = posts[i]
            if r0 in (16, 24):
                dsum[x, pl.ds(r0, 8)] += extra

    planes(2, STEP_X - 2, 2, step_2)

    def step_3(x):
        for r0 in (16, 24):
            posts, extra = step(2, s0, x, r0)
            for i in range(19):
                state_out[i, x - X0, pl.ds(r0 - Y0, 8)] = posts[i]
            total = dsum[x, pl.ds(r0, 8)] + extra
            sens[x - X0 + XF, pl.ds(r0, 8)] = heat0[x - X0, pl.ds(r0 - Y0, 8)] * total

    planes(3, STEP_X - 3, 4, step_3)

    for d in order:
        pl.when(exists(d))(lambda d=d: send(2, d))

    wait_recv(1)

    def weigh(x):
        for r0 in groups:
            rows = pl.ds(r0, 8)
            k = span0[x, rows]
            r2 = jnp.where(k == 0, 0.25, jnp.where(k == 1, 1.0, jnp.where(k == 2, 4.0, 16.0)))
            gain = jnp.where(k >= 0, 1.0 / (1.0 + 6.0 * r2), 0.0)
            gain_out[x, rows] = gain
            scale_out[x, rows] = gain * r2

    planes(0, FILTER_X, 4, weigh)

    wait_recv(2)
    for d in DIRS:

        @pl.when(exists(d))
        def _():
            for j in range(3):
                whole(j, d).wait_send()


def sweep_kernel(state, sens, scale, gain, state_out, smooth_out, own, q0, q1, sem):
    copy = pltpu.make_async_copy(state, state_out, sem)
    copy.start()
    lane = lax.broadcasted_iota(jnp.int32, (8, NZ), 1)
    for number in range(1, SWEEPS + 1):
        last = number == SWEEPS
        src = sens if number == 1 else (q0 if number % 2 == 0 else q1)
        dst = q0 if number % 2 == 1 else q1
        groups = (16, 24) if last else (8, 16, 24, 32)

        def sweep(x):
            for r0 in groups:
                rows = pl.ds(r0, 8)
                mid = src[x, rows]
                beside = src[x - 1, rows] + src[x + 1, rows]
                beside += src[x, pl.ds(r0 - 1, 8)] + src[x, pl.ds(r0 + 1, 8)]
                beside += jnp.where(lane == NZ - 1, 0.0, pltpu.roll(mid, NZ - 1, 1))
                beside += jnp.where(lane == 0, 0.0, pltpu.roll(mid, 1, 1))
                if number == 1:
                    base = mid * gain[x, rows]
                    own[x, rows] = base
                else:
                    base = own[x, rows]
                value = base + scale[x, rows] * beside
                if last:
                    smooth_out[x - XF, pl.ds(r0 - Y0, 8)] = value
                else:
                    dst[x, rows] = value

        planes(number, FILTER_X - number, FILTER_X, sweep)

    copy.wait()


def on_device(pop, vel, heat, obj, liq, span):
    f32, i32 = jnp.float32, jnp.int32
    vmem = pl.BlockSpec(memory_space=pltpu.VMEM)
    anywhere = pl.BlockSpec(memory_space=pltpu.HBM)
    frame = (FILTER_X, ROWS, NZ)
    step_frame = (STEP_X, ROWS, NZ)
    args = [
        pltpu.with_memory_space_constraint(x, pltpu.HBM)
        for x in (pop, vel, heat, obj, liq, span)
    ]
    state, sens, scale, gain = pl.pallas_call(
        exchange_kernel,
        out_shape=(
            jax.ShapeDtypeStruct((19, NX, NY, NZ), f32),
            jax.ShapeDtypeStruct(frame, f32),
            jax.ShapeDtypeStruct(frame, f32),
            jax.ShapeDtypeStruct(frame, f32),
        ),
        in_specs=[anywhere] * 6,
        out_specs=(vmem,) * 4,
        scratch_shapes=[
            pltpu.VMEM((19,) + step_frame, f32),
            pltpu.VMEM((19,) + step_frame, f32),
            pltpu.VMEM((3,) + step_frame, f32),
            pltpu.VMEM(step_frame, f32),
            pltpu.VMEM(step_frame, i32),
            pltpu.VMEM(frame, i32),
            pltpu.VMEM((NX, NY, NZ), f32),
            pltpu.VMEM((3,) + step_frame, f32),
            pltpu.VMEM(step_frame, f32),
            pltpu.VMEM(step_frame, f32),
            pltpu.VMEM(step_frame, f32),
            pltpu.VMEM((1024, NZ), f32),
            pltpu.SemaphoreType.DMA((6,)),
            pltpu.SemaphoreType.DMA((3, 8)),
            pltpu.SemaphoreType.DMA((3, 8)),
            pltpu.SemaphoreType.REGULAR,
        ],
        compiler_params=pltpu.CompilerParams(
            collective_id=0, has_side_effects=True, vmem_limit_bytes=36 << 20
        ),
        name="steps",
    )(*args)
    return pl.pallas_call(
        sweep_kernel,
        out_shape=(
            jax.ShapeDtypeStruct((19, NX, NY, NZ), f32),
            jax.ShapeDtypeStruct((NX, NY, NZ), f32),
        ),
        in_specs=[vmem] * 4,
        out_specs=(anywhere, vmem),
        scratch_shapes=[
            pltpu.VMEM(frame, f32),
            pltpu.VMEM(frame, f32),
            pltpu.VMEM(frame, f32),
            pltpu.SemaphoreType.DMA,
        ],
        compiler_params=pltpu.CompilerParams(vmem_limit_bytes=36 << 20),
        name="sweeps",
    )(state, sens, scale, gain)


def solution(mesh):
    field = P("grp", "blk", None)
    many = P(None, "grp", "blk", None)
    return jax.shard_map(
        on_device,
        mesh=mesh,
        in_specs=(many, many, field, field, field, field),
        out_specs=(many, field),
        check_vma=False,
    )
```

```python
import functools
import math

import jax
import jax.numpy as jnp
from jax import lax
from jax.experimental import pallas as pl
from jax.experimental.pallas import tpu as pltpu
from jax.sharding import PartitionSpec as P

MESH = pl.DeviceIdType.MESH
SWEEPS = 8
VELOCITIES = (
    (0, 0, 0),
    (1, 0, 0),
    (-1, 0, 0),
    (0, 1, 0),
    (0, -1, 0),
    (0, 0, 1),
    (0, 0, -1),
    (1, 1, 0),
    (-1, -1, 0),
    (1, -1, 0),
    (-1, 1, 0),
    (1, 0, 1),
    (-1, 0, -1),
    (1, 0, -1),
    (-1, 0, 1),
    (0, 1, 1),
    (0, -1, -1),
    (0, 1, -1),
    (0, -1, 1),
)
DIRS = ((1, 0), (-1, 0), (0, 1), (0, -1), (1, 1), (1, -1), (-1, 1), (-1, -1))
NX, NY, NZ = 8, 16, 128
X0, XF, Y0 = 3, 8, 16
ROWS = 48
STEP_X, FILTER_X = NX + 2 * X0, NX + 2 * XF
def src_span(side, length, first, last):
    if side > 0:
        return pl.ds(length - last, last - first + 1)
    if side < 0:
        return pl.ds(first - 1, last - first + 1)
    return pl.ds(0, length)


def dst_span(side, length, own, first, last):
    if side > 0:
        return pl.ds(own - last, last - first + 1)
    if side < 0:
        return pl.ds(own + length + first - 1, last - first + 1)
    return pl.ds(own, length)


def planes(first, end, together, body):
    main = (end - first) // together * together

    if main > together:

        @pl.loop(first, first + main, step=together)
        def _(x):
            for j in range(together):
                body(x + j)

    else:
        main = 0
    for x in range(first + main, end):
        body(x)


def runs_of(sx, sy):
    runs = []
    for i, (cx, cy, _) in enumerate(VELOCITIES):
        depth = (2 - sx * cx, 2 - sy * cy)
        if runs and runs[-1][2] == depth:
            runs[-1] = (runs[-1][0], runs[-1][1] + 1, depth)
        else:
            runs.append((i, 1, depth))
    return runs


def rows_in(*parts):
    return sum(math.prod(p.shape) // NZ for p in parts)


def exchange_kernel(
    pop, vel, heat, obj, liq, span,
    state_out, sens, scale_out, gain_out,
    s0, s1, u0, obj0, liq0, span0, heat0, um, ka, kb, extras, count,
    load_sem, ssem, rsem, ready,
):
    grp, blk = lax.axis_index("grp"), lax.axis_index("blk")
    n_grp, n_blk = lax.axis_size("grp"), lax.axis_size("blk")
    def exists(d):
        ok = None
        for side, at, n in ((d[0], grp, n_grp), (d[1], blk, n_blk)):
            if side:
                one = at < n - 1 if side > 0 else at > 0
                ok = one if ok is None else ok & one
        return ok

    def origin(d):
        return (grp + d[0] == 0) & (blk + d[1] == 0)

    def mutual(d):
        return ~origin((0, 0)) & ~origin(d)

    def first(d):
        if d[1] > 0:
            later = ~origin((0, 0))
        elif d[1] < 0:
            later = origin(d)
        else:
            later = origin(d) | (~origin((0, 0)) & (grp % 2 == 1))
        return later & ~mutual(d)

    def ahead(d):
        return exists(d) & ~first(d)

    def opposite(d):
        return (-d[0], -d[1])

    def peer(d):
        return dict(device_id=(grp + d[0], blk + d[1]), device_id_type=MESH)

    def remote(d, j, src, dst):
        k = DIRS.index(d)
        to = peer((d[0], 0)) if j == PASSED else peer(d)
        return pltpu.make_async_remote_copy(
            src_ref=src, dst_ref=dst, send_sem=ssem.at[j, k], recv_sem=rsem.at[j, k], **to
        )

    def part(d, src, dst, lead, depth, own_x, cut=None):
        xs, ys = src_span(d[0], NX, 1, depth[0]), src_span(d[1], NY, 1, depth[1])
        xd = dst_span(d[0], NX, own_x, 1, depth[0])
        yd = dst_span(d[1], NY, Y0, 1, depth[1])
        if cut:
            xs, xd = pl.ds(cut[0], cut[1]), pl.ds(own_x + cut[0], cut[1])
        return src.at[lead + (xs, ys)], dst.at[lead + (xd, yd)]

    def state_parts(d, cut):
        parts = [part(d, pop, s0, (pl.ds(a, n),), depth, X0, cut) for a, n, depth in runs_of(*d)]
        parts.append(part(d, vel, u0, (pl.ds(0, 3),), (2, 2), X0, cut))
        parts.append(part(d, obj, obj0, (), (2, 2), X0, cut))
        parts.append(part(d, liq, liq0, (), (2, 2), X0, cut))
        return parts

    even = grp % 2 == 0

    def rim_parts(d):
        return state_parts(d, None if d[0] else (jnp.where(even, 0, 3), NX - 3))

    def near_parts(d):
        return state_parts(d, (jnp.where(even, NX - 3, 0), 3))

    def passed_parts(d):
        dx, dy = d
        parts = []

        def add(frame, lead, depth):
            rows = dst_span(dy, NY, Y0, 1, depth[1])
            xs = src_span(dx, NX, 1, depth[0])
            xs, xd = pl.ds(X0 + xs.start, xs.size), dst_span(dx, NX, X0, 1, depth[0])
            parts.append((frame.at[lead + (xs, rows)], frame.at[lead + (xd, rows)]))

        for a, n, depth in runs_of(*d):
            add(s0, (pl.ds(a, n),), depth)
        add(u0, (pl.ds(0, 3),), (2, 2))
        add(obj0, (), (2, 2))
        add(liq0, (), (2, 2))
        return parts

    def direct(d):
        return (even if d[0] < 0 else ~even) if d[0] and d[1] else True

    def passes(d):
        return exists((0, -d[1])) & ~direct(d)

    def filter_pieces(d):
        dx, dy = d
        if dx and dy:
            near = ((1, 3, 1, 7), (4, 7, 1, 4))
        else:
            near = ((1, XF, 1, XF),)
        return [
            (src_span(dx, NX, a, b), src_span(dy, NY, c, e),
             dst_span(dx, NX, XF, a, b), dst_span(dy, NY, Y0, c, e))
            for a, b, c, e in near
        ]

    def span_parts(d):
        return [(span.at[xs, ys], span0.at[xd, yd]) for xs, ys, xd, yd in filter_pieces(d)]

    def sens_parts(d):
        pieces = filter_pieces(d)
        if not d[1]:
            xs, _, xd, _ = pieces[0]
            halves = (0, NY // 2), (NY // 2, NY // 2)
            pieces = [(xs, pl.ds(a, n), xd, pl.ds(Y0 + a, n)) for a, n in halves]
        return [
            (sens.at[pl.ds(xs.start + XF, xs.size), pl.ds(ys.start + Y0, ys.size)], sens.at[xd, yd])
            for xs, ys, xd, yd in pieces
        ]

    RIM, SPAN, SENS, NEAR, PASSED = range(5)
    stages = (rim_parts, span_parts, sens_parts, near_parts, passed_parts)

    def whole(j, d):
        rows = count.at[pl.ds(0, rows_in(*(src for src, _ in stages[j](d))))]
        return remote(d, j, rows, rows)

    def send(j, d, half=0):
        parts = stages[j](d)
        if j == SENS and not d[1]:
            parts = parts[half : half + 1]
        for src, dst in parts:
            remote(d, j, src, dst).start()

    def sends(j, d):
        return passes(d) if j == PASSED else exists(d) & direct(d) if j == RIM else exists(d)

    def gets(j, d):
        if j == PASSED:
            return exists((0, -d[1])) & direct(d)
        if j == RIM and d[0] and d[1]:
            return exists(opposite(d)) & ~direct(d)
        return exists(opposite(d))

    def directions(j):
        if j == NEAR:
            return ((0, 1), (0, -1))
        if j == PASSED:
            return ((1, 1), (1, -1), (-1, 1), (-1, -1))
        return DIRS

    def wait_recv(j):
        for d in directions(j):
            pl.when(gets(j, d))(lambda d=d: whole(j, d).wait_recv())

    def wait_send(j):
        for d in directions(j):
            pl.when(sends(j, d))(lambda d=d: whole(j, d).wait_send())

    barrier = pltpu.get_barrier_semaphore()
    expected = 0
    for d in DIRS:
        before = exists(d) & (first(d) | mutual(d))
        pl.when(before)(lambda d=d: pl.semaphore_signal(barrier, inc=1, **peer(d)))
        expected += jnp.where(ahead(d), 1, 0)
    pl.when(expected > 0)(lambda: pl.semaphore_wait(barrier, expected))

    corners = ((1, 1), (1, -1), (-1, 1), (-1, -1))
    order = corners + ((1, 0), (-1, 0), (0, 1), (0, -1))
    work = [(RIM, d) for d in order[4:6] + corners] + [(NEAR, (0, 1)), (NEAR, (0, -1))]
    work += [(RIM, d) for d in order[6:]]

    def greet(d):
        pl.semaphore_signal(ready.at[DIRS.index(d)], inc=1, **peer(d))

    for d in order:
        pl.when(ahead(d) & ~mutual(d))(lambda d=d: greet(d))
    for j, d in work:
        pl.when(ahead(d) & sends(j, d))(lambda j=j, d=d: send(j, d))

    own = (pl.ds(X0, NX), pl.ds(Y0, NY))
    loads = [
        pltpu.make_async_copy(src, dst, load_sem.at[j])
        for j, (src, dst) in enumerate(
            (
                (pop, s0.at[(pl.ds(0, 19),) + own]),
                (vel, u0.at[(pl.ds(0, 3),) + own]),
                (obj, obj0.at[own]),
                (liq, liq0.at[own]),
                (heat, heat0),
                (span, span0.at[pl.ds(XF, NX), pl.ds(Y0, NY)]),
            )
        )
    ]
    for c in loads:
        c.start()

    for d in ((1, 0), (-1, 0), (1, 1), (-1, 1), (0, 1), (0, -1), (-1, -1)):

        @pl.when(exists(d) & first(d))
        def _():
            pl.semaphore_wait(ready.at[DIRS.index(opposite(d))], 1)
            for j, to in work:
                if to == d:
                    pl.when(sends(j, d))(lambda j=j, d=d: send(j, d))

    def outside(x_step, x_filter, rows):
        def fill(first, count, width, put):
            @pl.loop(first, first + count)
            def _(x):
                for r in rows:
                    put(x, pl.ds(r, 8))

        zero = jnp.zeros((8, NZ), jnp.float32)
        none = jnp.full((8, NZ), -1, jnp.int32)

        def put_step(x, r):
            for i in range(19):
                s0[i, x, r] = zero
            for i in range(3):
                u0[i, x, r] = zero
            obj0[x, r] = zero
            liq0[x, r] = none

        def put_filter(x, r):
            span0[x, r] = none
            sens[x, r] = zero

        fill(*x_step, None, put_step)
        fill(*x_filter, None, put_filter)

    groups = (8, 16, 24, 32)
    pl.when(grp == 0)(lambda: outside((0, X0), (0, XF), groups))
    pl.when(grp == n_grp - 1)(lambda: outside((X0 + NX, X0), (XF + NX, XF), groups))
    pl.when(blk == 0)(lambda: outside((0, STEP_X), (0, FILTER_X), (8,)))
    pl.when(blk == n_blk - 1)(lambda: outside((0, STEP_X), (0, FILTER_X), (32,)))

    wait_recv(NEAR)
    for d in corners:
        pl.when(passes(d))(lambda d=d: send(PASSED, d))
    for d in order:
        pl.when(exists(d))(lambda d=d: send(SPAN, d))
    for c in loads:
        c.wait()
    lane = lax.broadcasted_iota(jnp.int32, (8, NZ), 1)

    def step(number, src, x, r0):
        def pulled(i):
            cx, cy, cz = VELOCITIES[i]
            v = src[i, x + cx, pl.ds(r0 + cy, 8)]
            if cz > 0:
                return jnp.where(lane == NZ - 1, 0.0, pltpu.roll(v, NZ - 1, 1))
            if cz < 0:
                return jnp.where(lane == 0, 0.0, pltpu.roll(v, 1, 1))
            return v

        p = [pulled(i) for i in range(19)]
        rows = pl.ds(r0, 8)
        if number == 0:
            kind = liq0[x, rows]
            fluid = kind.astype(jnp.float32)
            inside = kind >= 0
            omega = 0.9 + 0.7 * fluid
            b = jnp.where(inside, omega, 0.0)
            a = jnp.where(inside, 1.0 - omega, 0.0)
            third = fluid * (3.0 / 36.0)
            ux, uy, uz = (u0[i, x, rows] * third for i in range(3))
            ka[x, rows] = a
            kb[x, rows] = b
            um[0, x, rows] = ux
            um[1, x, rows] = uy
            um[2, x, rows] = uz
        else:
            a, b = ka[x, rows], kb[x, rows]
            ux, uy, uz = (um[i, x, rows] for i in range(3))
        total = {i: p[i] + p[i + 1] for i in range(1, 19, 2)}
        diff = {i: p[i] - p[i + 1] for i in range(1, 19, 2)}
        faces = total[1] + total[3] + total[5]
        edges = (total[7] + total[9]) + (total[11] + total[13]) + (total[15] + total[17])
        average = p[0] * (1.0 / 3.0) + faces * (1.0 / 18.0) + edges * (1.0 / 36.0)
        mx = (diff[1] + diff[1]) + (diff[7] + diff[9]) + (diff[11] + diff[13])
        my = (diff[3] + diff[3]) + (diff[7] - diff[9]) + (diff[15] + diff[17])
        mz = (diff[5] + diff[5]) + (diff[11] - diff[13]) + (diff[15] - diff[17])
        extra = ux * mx + uy * my + uz * mz
        pushed = b * (average + extra)
        o = obj0[x, rows] * (1.0 / 36.0)
        o2 = o + o
        adds = (pushed + 12.0 * o, pushed + o2, pushed + o)
        return [a * p[i] + adds[0 if i == 0 else 1 if i < 7 else 2] for i in range(19)], extra

    def step_1(starts, x):
        for r0 in starts:
            rows = pl.ds(r0, 8)
            posts, extra = step(0, s0, x, r0)
            for i in range(19):
                s1[i, x, rows] = posts[i]
            extras[0, x, rows] = extra

    def step_2(starts, x):
        for r0 in starts:
            rows = pl.ds(r0, 8)
            posts, extra = step(1, s1, x, r0)
            for i in range(19):
                s0[i, x, rows] = posts[i]
            extras[1, x, rows] = extra

    def step_3(starts, x):
        for r0 in starts:
            rows, here = pl.ds(r0, 8), pl.ds(r0 - Y0, 8)
            posts, extra = step(2, s0, x, r0)
            for i in range(19):
                state_out[i, x - X0, here] = posts[i]
            total = extras[0, x, rows] + extras[1, x, rows] + extra
            sens[x - X0 + XF, rows] = heat0[x - X0, here] * total

    for side in (1, -1):
        low = side > 0
        for j in (RIM, PASSED):
            for d in directions(j):
                if d[1] == side or (low and d[1] == 0):
                    pl.when(gets(j, d))(lambda j=j, d=d: whole(j, d).wait_recv())
        starts = ((Y0 - 2, Y0 + 2), (Y0 - 1, Y0 + 1), (Y0,)) if low else ((Y0 + 10,), (Y0 + 9,), (Y0 + 8,))
        planes(1, STEP_X - 1, 4 if low else 6, functools.partial(step_1, starts[0]))
        for d in corners:
            if d[1] == side:
                pl.when(sends(PASSED, d))(lambda d=d: whole(PASSED, d).wait_send())
        planes(2, STEP_X - 2, 5, functools.partial(step_2, starts[1]))
        planes(3, STEP_X - 3, 8, functools.partial(step_3, starts[2]))
        for d in order:
            if d[1] in (0, -side):
                pl.when(exists(d))(lambda d=d: send(SENS, d, 0 if low else 1))

    wait_recv(SPAN)

    def weigh(x):
        for r0 in groups:
            rows = pl.ds(r0, 8)
            k = span0[x, rows]
            r2 = jnp.where(k == 0, 0.25, jnp.where(k == 1, 1.0, jnp.where(k == 2, 4.0, 16.0)))
            gain = jnp.where(k >= 0, 1.0 / (1.0 + 6.0 * r2), 0.0)
            gain_out[x, rows] = gain
            scale_out[x, rows] = gain * r2

    planes(0, FILTER_X, 4, weigh)

    wait_recv(SENS)
    for j in (RIM, SPAN, SENS, NEAR):
        wait_send(j)


def sweep_kernel(state, sens, scale, gain, state_out, smooth_out, own, q0, q1, smooth, sem):
    copies = (
        pltpu.make_async_copy(state, state_out, sem.at[0]),
        pltpu.make_async_copy(smooth, smooth_out, sem.at[1]),
    )
    copies[0].start()
    lane = lax.broadcasted_iota(jnp.int32, (8, NZ), 1)
    for number in range(1, SWEEPS + 1):
        last = number == SWEEPS
        src = sens if number == 1 else (q0 if number % 2 == 0 else q1)
        dst = q0 if number % 2 == 1 else q1
        reach = SWEEPS - number
        for x in range(number, FILTER_X - number):
            over = max(XF - x, x - XF - NX + 1, 0)
            low, high = Y0 - (reach - over), Y0 + NY + (reach - over)
            for r0 in list(range(low, high - 8, 8)) + [high - 8]:
                rows = pl.ds(r0, 8)
                mid = src[x, rows]
                beside = src[x - 1, rows] + src[x + 1, rows]
                beside += src[x, pl.ds(r0 - 1, 8)] + src[x, pl.ds(r0 + 1, 8)]
                beside += jnp.where(lane == NZ - 1, 0.0, pltpu.roll(mid, NZ - 1, 1))
                beside += jnp.where(lane == 0, 0.0, pltpu.roll(mid, 1, 1))
                if number == 1:
                    base = mid * gain[x, rows]
                    own[x, rows] = base
                else:
                    base = own[x, rows]
                value = base + scale[x, rows] * beside
                if last:
                    smooth[x - XF, pl.ds(r0 - Y0, 8)] = value
                else:
                    dst[x, rows] = value

    copies[1].start()
    for c in copies:
        c.wait()


def on_device(pop, vel, heat, obj, liq, span):
    f32, i32 = jnp.float32, jnp.int32
    vmem = pl.BlockSpec(memory_space=pltpu.VMEM)
    anywhere = pl.BlockSpec(memory_space=pltpu.HBM)
    frame = (FILTER_X, ROWS, NZ)
    step_frame = (STEP_X, ROWS, NZ)
    args = [
        pltpu.with_memory_space_constraint(x, pltpu.HBM)
        for x in (pop, vel, heat, obj, liq, span)
    ]
    state, sens, scale, gain = pl.pallas_call(
        exchange_kernel,
        out_shape=(
            jax.ShapeDtypeStruct((19, NX, NY, NZ), f32),
            jax.ShapeDtypeStruct(frame, f32),
            jax.ShapeDtypeStruct(frame, f32),
            jax.ShapeDtypeStruct(frame, f32),
        ),
        in_specs=[anywhere] * 6,
        out_specs=(vmem,) * 4,
        scratch_shapes=[
            pltpu.VMEM((19,) + step_frame, f32),
            pltpu.VMEM((19,) + step_frame, f32),
            pltpu.VMEM((3,) + step_frame, f32),
            pltpu.VMEM(step_frame, f32),
            pltpu.VMEM(step_frame, i32),
            pltpu.VMEM(frame, i32),
            pltpu.VMEM((NX, NY, NZ), f32),
            pltpu.VMEM((3,) + step_frame, f32),
            pltpu.VMEM(step_frame, f32),
            pltpu.VMEM(step_frame, f32),
            pltpu.VMEM((2,) + step_frame, f32),
            pltpu.VMEM((1024, NZ), f32),
            pltpu.SemaphoreType.DMA((6,)),
            pltpu.SemaphoreType.DMA((5, 8)),
            pltpu.SemaphoreType.DMA((5, 8)),
            pltpu.SemaphoreType.REGULAR((8,)),
        ],
        compiler_params=pltpu.CompilerParams(
            collective_id=0, has_side_effects=True, vmem_limit_bytes=36 << 20
        ),
        name="steps",
    )(*args)
    return pl.pallas_call(
        sweep_kernel,
        out_shape=(
            jax.ShapeDtypeStruct((19, NX, NY, NZ), f32),
            jax.ShapeDtypeStruct((NX, NY, NZ), f32),
        ),
        in_specs=[vmem] * 4,
        out_specs=(anywhere, anywhere),
        scratch_shapes=[
            pltpu.VMEM(frame, f32),
            pltpu.VMEM(frame, f32),
            pltpu.VMEM(frame, f32),
            pltpu.VMEM((NX, NY, NZ), f32),
            pltpu.SemaphoreType.DMA((2,)),
        ],
        compiler_params=pltpu.CompilerParams(vmem_limit_bytes=36 << 20),
        name="sweeps",
    )(state, sens, scale, gain)


def solution(mesh):
    field = P("grp", "blk", None)
    many = P(None, "grp", "blk", None)
    return jax.shard_map(
        on_device,
        mesh=mesh,
        in_specs=(many, many, field, field, field, field),
        out_specs=(many, field),
        check_vma=False,
    )
```

```python
import functools
import math

import jax
import jax.numpy as jnp
from jax import lax
from jax.experimental import pallas as pl
from jax.experimental.pallas import tpu as pltpu
from jax.sharding import PartitionSpec as P

MESH = pl.DeviceIdType.MESH
SWEEPS = 8
VELOCITIES = (
    (0, 0, 0),
    (1, 0, 0),
    (-1, 0, 0),
    (0, 1, 0),
    (0, -1, 0),
    (0, 0, 1),
    (0, 0, -1),
    (1, 1, 0),
    (-1, -1, 0),
    (1, -1, 0),
    (-1, 1, 0),
    (1, 0, 1),
    (-1, 0, -1),
    (1, 0, -1),
    (-1, 0, 1),
    (0, 1, 1),
    (0, -1, -1),
    (0, 1, -1),
    (0, -1, 1),
)
DIRS = ((1, 0), (-1, 0), (0, 1), (0, -1), (1, 1), (1, -1), (-1, 1), (-1, -1))
NX, NY, NZ = 8, 16, 128
X0, XF, Y0 = 3, 8, 16
ROWS = 48
LOW_ROWS = 11
STEP_X, FILTER_X = NX + 2 * X0, NX + 2 * XF
def src_span(side, length, first, last):
    if side > 0:
        return pl.ds(length - last, last - first + 1)
    if side < 0:
        return pl.ds(first - 1, last - first + 1)
    return pl.ds(0, length)


def dst_span(side, length, own, first, last):
    if side > 0:
        return pl.ds(own - last, last - first + 1)
    if side < 0:
        return pl.ds(own + length + first - 1, last - first + 1)
    return pl.ds(own, length)


def planes(first, end, together, body):
    main = (end - first) // together * together

    if main > together:

        @pl.loop(first, first + main, step=together)
        def _(x):
            for j in range(together):
                body(x + j)

    else:
        main = 0
    for x in range(first + main, end):
        body(x)


def runs_of(sx, sy):
    runs = []
    for i, (cx, cy, _) in enumerate(VELOCITIES):
        depth = (2 - sx * cx, 2 - sy * cy)
        if runs and runs[-1][2] == depth:
            runs[-1] = (runs[-1][0], runs[-1][1] + 1, depth)
        else:
            runs.append((i, 1, depth))
    return runs


def rows_in(*parts):
    return sum(math.prod(p.shape) // NZ for p in parts)


def exchange_kernel(
    pop, vel, heat, obj, liq, span,
    state_out, sens, scale_out, gain_out,
    s0, s1, u0, obj0, liq0, span0, heat0, um, ka, kb, extras, count,
    load_sem, ssem, rsem, ready,
):
    grp, blk = lax.axis_index("grp"), lax.axis_index("blk")
    n_grp, n_blk = lax.axis_size("grp"), lax.axis_size("blk")
    def exists(d):
        ok = None
        for side, at, n in ((d[0], grp, n_grp), (d[1], blk, n_blk)):
            if side:
                one = at < n - 1 if side > 0 else at > 0
                ok = one if ok is None else ok & one
        return ok

    def origin(d):
        return (grp + d[0] == 0) & (blk + d[1] == 0)

    def mutual(d):
        return ~origin((0, 0)) & ~origin(d)

    def first(d):
        if d[1] > 0:
            later = ~origin((0, 0))
        elif d[1] < 0:
            later = origin(d)
        else:
            later = origin(d) | (~origin((0, 0)) & (grp % 2 == 1))
        return later & ~mutual(d)

    def ahead(d):
        return exists(d) & ~first(d)

    def opposite(d):
        return (-d[0], -d[1])

    def peer(d):
        return dict(device_id=(grp + d[0], blk + d[1]), device_id_type=MESH)

    def remote(d, j, src, dst):
        k = DIRS.index(d)
        to = peer((d[0], 0)) if j == PASSED else peer(d)
        return pltpu.make_async_remote_copy(
            src_ref=src, dst_ref=dst, send_sem=ssem.at[j, k], recv_sem=rsem.at[j, k], **to
        )

    def part(d, src, dst, lead, depth, own_x, cut=None, rows=None):
        xs, ys = src_span(d[0], NX, 1, depth[0]), src_span(d[1], NY, 1, depth[1])
        xd = dst_span(d[0], NX, own_x, 1, depth[0])
        yd = dst_span(d[1], NY, Y0, 1, depth[1])
        if cut:
            xs, xd = pl.ds(cut[0], cut[1]), pl.ds(own_x + cut[0], cut[1])
        if rows:
            ys, yd = pl.ds(rows[0], rows[1]), pl.ds(Y0 + rows[0], rows[1])
        return src.at[lead + (xs, ys)], dst.at[lead + (xd, yd)]

    def state_parts(d, *cuts):
        parts = [part(d, pop, s0, (pl.ds(a, n),), depth, X0, *cuts) for a, n, depth in runs_of(*d)]
        parts.append(part(d, vel, u0, (pl.ds(0, 3),), (2, 2), X0, *cuts))
        parts.append(part(d, obj, obj0, (), (2, 2), X0, *cuts))
        parts.append(part(d, liq, liq0, (), (2, 2), X0, *cuts))
        return parts

    even = grp % 2 == 0

    def rim_parts(d):
        if not d[0]:
            return state_parts(d, (jnp.where(even, 0, 3), NX - 3))
        return state_parts(d, None, None if d[1] else (0, LOW_ROWS))

    def upper_parts(d):
        return state_parts(d, None, (LOW_ROWS, NY - LOW_ROWS))

    def near_parts(d):
        return state_parts(d, (jnp.where(even, NX - 3, 0), 3))

    def passed_parts(d):
        dx, dy = d
        parts = []

        def add(frame, lead, depth):
            rows = dst_span(dy, NY, Y0, 1, depth[1])
            xs = src_span(dx, NX, 1, depth[0])
            xs, xd = pl.ds(X0 + xs.start, xs.size), dst_span(dx, NX, X0, 1, depth[0])
            parts.append((frame.at[lead + (xs, rows)], frame.at[lead + (xd, rows)]))

        for a, n, depth in runs_of(*d):
            add(s0, (pl.ds(a, n),), depth)
        add(u0, (pl.ds(0, 3),), (2, 2))
        add(obj0, (), (2, 2))
        add(liq0, (), (2, 2))
        return parts

    def direct(d):
        return (even if d[0] < 0 else ~even) if d[0] and d[1] else True

    def passes(d):
        return exists((0, -d[1])) & ~direct(d)

    def filter_pieces(d):
        dx, dy = d
        if dx and dy:
            near = ((1, 3, 1, 7), (4, 7, 1, 4))
        else:
            near = ((1, XF, 1, XF),)
        return [
            (src_span(dx, NX, a, b), src_span(dy, NY, c, e),
             dst_span(dx, NX, XF, a, b), dst_span(dy, NY, Y0, c, e))
            for a, b, c, e in near
        ]

    def span_parts(d):
        return [(span.at[xs, ys], span0.at[xd, yd]) for xs, ys, xd, yd in filter_pieces(d)]

    def sens_parts(d):
        pieces = filter_pieces(d)
        if not d[1]:
            xs, _, xd, _ = pieces[0]
            halves = (0, NY // 2), (NY // 2, NY // 2)
            pieces = [(xs, pl.ds(a, n), xd, pl.ds(Y0 + a, n)) for a, n in halves]
        return [
            (sens.at[pl.ds(xs.start + XF, xs.size), pl.ds(ys.start + Y0, ys.size)], sens.at[xd, yd])
            for xs, ys, xd, yd in pieces
        ]

    RIM, SPAN, SENS, NEAR, PASSED, UPPER = range(6)
    stages = (rim_parts, span_parts, sens_parts, near_parts, passed_parts, upper_parts)

    def whole(j, d):
        rows = count.at[pl.ds(0, rows_in(*(src for src, _ in stages[j](d))))]
        return remote(d, j, rows, rows)

    def send(j, d, half=0):
        parts = stages[j](d)
        if j == SENS and not d[1]:
            parts = parts[half : half + 1]
        for src, dst in parts:
            remote(d, j, src, dst).start()

    def sends(j, d):
        return passes(d) if j == PASSED else exists(d) & direct(d) if j == RIM else exists(d)

    def gets(j, d):
        if j == PASSED:
            return exists((0, -d[1])) & direct(d)
        if j == RIM and d[0] and d[1]:
            return exists(opposite(d)) & ~direct(d)
        return exists(opposite(d))

    def directions(j):
        if j == NEAR:
            return ((0, 1), (0, -1))
        if j == UPPER:
            return ((1, 0), (-1, 0))
        if j == PASSED:
            return ((1, 1), (1, -1), (-1, 1), (-1, -1))
        return DIRS

    def wait_recv(j):
        for d in directions(j):
            pl.when(gets(j, d))(lambda d=d: whole(j, d).wait_recv())

    def wait_send(j):
        for d in directions(j):
            pl.when(sends(j, d))(lambda d=d: whole(j, d).wait_send())

    barrier = pltpu.get_barrier_semaphore()
    expected = 0
    for d in DIRS:
        before = exists(d) & (first(d) | mutual(d))
        pl.when(before)(lambda d=d: pl.semaphore_signal(barrier, inc=1, **peer(d)))
        expected += jnp.where(ahead(d), 1, 0)
    pl.when(expected > 0)(lambda: pl.semaphore_wait(barrier, expected))

    corners = ((1, 1), (1, -1), (-1, 1), (-1, -1))
    order = corners + ((1, 0), (-1, 0), (0, 1), (0, -1))
    work = [(RIM, d) for d in ((1, 1), (-1, 1), (1, 0), (-1, 0))] + [(NEAR, (0, 1)), (NEAR, (0, -1))]
    work += [(UPPER, (1, 0)), (UPPER, (-1, 0)), (RIM, (1, -1)), (RIM, (-1, -1))]
    work += [(RIM, (0, 1)), (RIM, (0, -1))]

    def greet(d):
        pl.semaphore_signal(ready.at[DIRS.index(d)], inc=1, **peer(d))

    for d in order:
        pl.when(ahead(d) & ~mutual(d))(lambda d=d: greet(d))
    for j, d in work:
        pl.when(ahead(d) & sends(j, d))(lambda j=j, d=d: send(j, d))

    own = (pl.ds(X0, NX), pl.ds(Y0, NY))
    loads = [
        pltpu.make_async_copy(src, dst, load_sem.at[j])
        for j, (src, dst) in enumerate(
            (
                (pop, s0.at[(pl.ds(0, 19),) + own]),
                (vel, u0.at[(pl.ds(0, 3),) + own]),
                (obj, obj0.at[own]),
                (liq, liq0.at[own]),
                (heat, heat0),
                (span, span0.at[pl.ds(XF, NX), pl.ds(Y0, NY)]),
            )
        )
    ]
    for c in loads:
        c.start()

    for d in ((1, 0), (-1, 0), (1, 1), (-1, 1), (0, 1), (0, -1), (-1, -1)):

        @pl.when(exists(d) & first(d))
        def _():
            pl.semaphore_wait(ready.at[DIRS.index(opposite(d))], 1)
            for j, to in work:
                if to == d:
                    pl.when(sends(j, d))(lambda j=j, d=d: send(j, d))

    def outside(x_step, x_filter, rows):
        def fill(first, count, width, put):
            @pl.loop(first, first + count)
            def _(x):
                for r in rows:
                    put(x, pl.ds(r, 8))

        zero = jnp.zeros((8, NZ), jnp.float32)
        none = jnp.full((8, NZ), -1, jnp.int32)

        def put_step(x, r):
            for i in range(19):
                s0[i, x, r] = zero
            for i in range(3):
                u0[i, x, r] = zero
            obj0[x, r] = zero
            liq0[x, r] = none

        def put_filter(x, r):
            span0[x, r] = none
            sens[x, r] = zero

        fill(*x_step, None, put_step)
        fill(*x_filter, None, put_filter)

    groups = (8, 16, 24, 32)
    pl.when(grp == 0)(lambda: outside((0, X0), (0, XF), groups))
    pl.when(grp == n_grp - 1)(lambda: outside((X0 + NX, X0), (XF + NX, XF), groups))
    pl.when(blk == 0)(lambda: outside((0, STEP_X), (0, FILTER_X), (8,)))
    pl.when(blk == n_blk - 1)(lambda: outside((0, STEP_X), (0, FILTER_X), (32,)))

    wait_recv(NEAR)
    for d in corners:
        pl.when(passes(d))(lambda d=d: send(PASSED, d))
    for d in order:
        pl.when(exists(d))(lambda d=d: send(SPAN, d))
    for c in loads:
        c.wait()
    lane = lax.broadcasted_iota(jnp.int32, (8, NZ), 1)

    def step(number, src, x, r0):
        def pulled(i):
            cx, cy, cz = VELOCITIES[i]
            v = src[i, x + cx, pl.ds(r0 + cy, 8)]
            if cz > 0:
                return jnp.where(lane == NZ - 1, 0.0, pltpu.roll(v, NZ - 1, 1))
            if cz < 0:
                return jnp.where(lane == 0, 0.0, pltpu.roll(v, 1, 1))
            return v

        p = [pulled(i) for i in range(19)]
        rows = pl.ds(r0, 8)
        if number == 0:
            kind = liq0[x, rows]
            fluid = kind.astype(jnp.float32)
            inside = kind >= 0
            omega = 0.9 + 0.7 * fluid
            b = jnp.where(inside, omega, 0.0)
            a = jnp.where(inside, 1.0 - omega, 0.0)
            third = fluid * (3.0 / 36.0)
            ux, uy, uz = (u0[i, x, rows] * third for i in range(3))
            ka[x, rows] = a
            kb[x, rows] = b
            um[0, x, rows] = ux
            um[1, x, rows] = uy
            um[2, x, rows] = uz
        else:
            a, b = ka[x, rows], kb[x, rows]
            ux, uy, uz = (um[i, x, rows] for i in range(3))
        total = {i: p[i] + p[i + 1] for i in range(1, 19, 2)}
        diff = {i: p[i] - p[i + 1] for i in range(1, 19, 2)}
        faces = total[1] + total[3] + total[5]
        edges = (total[7] + total[9]) + (total[11] + total[13]) + (total[15] + total[17])
        average = p[0] * (1.0 / 3.0) + faces * (1.0 / 18.0) + edges * (1.0 / 36.0)
        mx = (diff[1] + diff[1]) + (diff[7] + diff[9]) + (diff[11] + diff[13])
        my = (diff[3] + diff[3]) + (diff[7] - diff[9]) + (diff[15] + diff[17])
        mz = (diff[5] + diff[5]) + (diff[11] - diff[13]) + (diff[15] - diff[17])
        extra = ux * mx + uy * my + uz * mz
        pushed = b * (average + extra)
        o = obj0[x, rows] * (1.0 / 36.0)
        o2 = o + o
        adds = (pushed + 12.0 * o, pushed + o2, pushed + o)
        return [a * p[i] + adds[0 if i == 0 else 1 if i < 7 else 2] for i in range(19)], extra

    def step_1(starts, x):
        for r0 in starts:
            rows = pl.ds(r0, 8)
            posts, extra = step(0, s0, x, r0)
            for i in range(19):
                s1[i, x, rows] = posts[i]
            extras[0, x, rows] = extra

    def step_2(starts, x):
        for r0 in starts:
            rows = pl.ds(r0, 8)
            posts, extra = step(1, s1, x, r0)
            for i in range(19):
                s0[i, x, rows] = posts[i]
            extras[1, x, rows] = extra

    def step_3(starts, x):
        for r0 in starts:
            rows, here = pl.ds(r0, 8), pl.ds(r0 - Y0, 8)
            posts, extra = step(2, s0, x, r0)
            for i in range(19):
                state_out[i, x - X0, here] = posts[i]
            total = extras[0, x, rows] + extras[1, x, rows] + extra
            sens[x - X0 + XF, rows] = heat0[x - X0, here] * total

    for side in (1, -1):
        low = side > 0
        for j in (RIM, PASSED, UPPER):
            for d in directions(j):
                if d[1] == side or (d[1] == 0 and low == (j == RIM)):
                    pl.when(gets(j, d))(lambda j=j, d=d: whole(j, d).wait_recv())
        starts = ((Y0 - 2, Y0 + 2), (Y0 - 1, Y0 + 1), (Y0,)) if low else ((Y0 + 10,), (Y0 + 9,), (Y0 + 8,))
        planes(1, STEP_X - 1, 4 if low else 6, functools.partial(step_1, starts[0]))
        for d in corners:
            if d[1] == side:
                pl.when(sends(PASSED, d))(lambda d=d: whole(PASSED, d).wait_send())
        planes(2, STEP_X - 2, 5, functools.partial(step_2, starts[1]))
        planes(3, STEP_X - 3, 8, functools.partial(step_3, starts[2]))
        for d in order:
            if d[1] in (0, -side):
                pl.when(exists(d))(lambda d=d: send(SENS, d, 0 if low else 1))

    wait_recv(SPAN)

    def weigh(x):
        for r0 in groups:
            rows = pl.ds(r0, 8)
            k = span0[x, rows]
            r2 = jnp.where(k == 0, 0.25, jnp.where(k == 1, 1.0, jnp.where(k == 2, 4.0, 16.0)))
            gain = jnp.where(k >= 0, 1.0 / (1.0 + 6.0 * r2), 0.0)
            gain_out[x, rows] = gain
            scale_out[x, rows] = gain * r2

    planes(0, FILTER_X, 4, weigh)

    wait_recv(SENS)
    for j in (RIM, SPAN, SENS, NEAR, UPPER):
        wait_send(j)


def sweep_kernel(state, sens, scale, gain, state_out, smooth_out, own, q0, q1, smooth, sem):
    copies = (
        pltpu.make_async_copy(state, state_out, sem.at[0]),
        pltpu.make_async_copy(smooth, smooth_out, sem.at[1]),
    )
    copies[0].start()
    lane = lax.broadcasted_iota(jnp.int32, (8, NZ), 1)
    for number in range(1, SWEEPS + 1):
        last = number == SWEEPS
        src = sens if number == 1 else (q0 if number % 2 == 0 else q1)
        dst = q0 if number % 2 == 1 else q1
        reach = SWEEPS - number
        for x in range(number, FILTER_X - number):
            over = max(XF - x, x - XF - NX + 1, 0)
            low, high = Y0 - (reach - over), Y0 + NY + (reach - over)
            for r0 in list(range(low, high - 8, 8)) + [high - 8]:
                rows = pl.ds(r0, 8)
                mid = src[x, rows]
                beside = src[x - 1, rows] + src[x + 1, rows]
                beside += src[x, pl.ds(r0 - 1, 8)] + src[x, pl.ds(r0 + 1, 8)]
                beside += jnp.where(lane == NZ - 1, 0.0, pltpu.roll(mid, NZ - 1, 1))
                beside += jnp.where(lane == 0, 0.0, pltpu.roll(mid, 1, 1))
                if number == 1:
                    base = mid * gain[x, rows]
                    own[x, rows] = base
                else:
                    base = own[x, rows]
                value = base + scale[x, rows] * beside
                if last:
                    smooth[x - XF, pl.ds(r0 - Y0, 8)] = value
                else:
                    dst[x, rows] = value

    copies[1].start()
    for c in copies:
        c.wait()


def on_device(pop, vel, heat, obj, liq, span):
    f32, i32 = jnp.float32, jnp.int32
    vmem = pl.BlockSpec(memory_space=pltpu.VMEM)
    anywhere = pl.BlockSpec(memory_space=pltpu.HBM)
    frame = (FILTER_X, ROWS, NZ)
    step_frame = (STEP_X, ROWS, NZ)
    args = [
        pltpu.with_memory_space_constraint(x, pltpu.HBM)
        for x in (pop, vel, heat, obj, liq, span)
    ]
    state, sens, scale, gain = pl.pallas_call(
        exchange_kernel,
        out_shape=(
            jax.ShapeDtypeStruct((19, NX, NY, NZ), f32),
            jax.ShapeDtypeStruct(frame, f32),
            jax.ShapeDtypeStruct(frame, f32),
            jax.ShapeDtypeStruct(frame, f32),
        ),
        in_specs=[anywhere] * 6,
        out_specs=(vmem,) * 4,
        scratch_shapes=[
            pltpu.VMEM((19,) + step_frame, f32),
            pltpu.VMEM((19,) + step_frame, f32),
            pltpu.VMEM((3,) + step_frame, f32),
            pltpu.VMEM(step_frame, f32),
            pltpu.VMEM(step_frame, i32),
            pltpu.VMEM(frame, i32),
            pltpu.VMEM((NX, NY, NZ), f32),
            pltpu.VMEM((3,) + step_frame, f32),
            pltpu.VMEM(step_frame, f32),
            pltpu.VMEM(step_frame, f32),
            pltpu.VMEM((2,) + step_frame, f32),
            pltpu.VMEM((1024, NZ), f32),
            pltpu.SemaphoreType.DMA((6,)),
            pltpu.SemaphoreType.DMA((6, 8)),
            pltpu.SemaphoreType.DMA((6, 8)),
            pltpu.SemaphoreType.REGULAR((8,)),
        ],
        compiler_params=pltpu.CompilerParams(
            collective_id=0, has_side_effects=True, vmem_limit_bytes=36 << 20
        ),
        name="steps",
    )(*args)
    return pl.pallas_call(
        sweep_kernel,
        out_shape=(
            jax.ShapeDtypeStruct((19, NX, NY, NZ), f32),
            jax.ShapeDtypeStruct((NX, NY, NZ), f32),
        ),
        in_specs=[vmem] * 4,
        out_specs=(anywhere, anywhere),
        scratch_shapes=[
            pltpu.VMEM(frame, f32),
            pltpu.VMEM(frame, f32),
            pltpu.VMEM(frame, f32),
            pltpu.VMEM((NX, NY, NZ), f32),
            pltpu.SemaphoreType.DMA((2,)),
        ],
        compiler_params=pltpu.CompilerParams(vmem_limit_bytes=36 << 20),
        name="sweeps",
    )(state, sens, scale, gain)


def solution(mesh):
    field = P("grp", "blk", None)
    many = P(None, "grp", "blk", None)
    return jax.shard_map(
        on_device,
        mesh=mesh,
        in_specs=(many, many, field, field, field, field),
        out_specs=(many, field),
        check_vma=False,
    )
```

```python
import functools
import math

import jax
import jax.numpy as jnp
from jax import lax
from jax.experimental import pallas as pl
from jax.experimental.pallas import tpu as pltpu
from jax.sharding import PartitionSpec as P

MESH = pl.DeviceIdType.MESH
SWEEPS = 8
VELOCITIES = (
    (0, 0, 0),
    (1, 0, 0),
    (-1, 0, 0),
    (0, 1, 0),
    (0, -1, 0),
    (0, 0, 1),
    (0, 0, -1),
    (1, 1, 0),
    (-1, -1, 0),
    (1, -1, 0),
    (-1, 1, 0),
    (1, 0, 1),
    (-1, 0, -1),
    (1, 0, -1),
    (-1, 0, 1),
    (0, 1, 1),
    (0, -1, -1),
    (0, 1, -1),
    (0, -1, 1),
)
DIRS = ((1, 0), (-1, 0), (0, 1), (0, -1), (1, 1), (1, -1), (-1, 1), (-1, -1))
NX, NY, NZ = 8, 16, 128
X0, XF, Y0 = 3, 8, 16
ROWS = 48
LOW_ROWS = 11
STEP_X, FILTER_X = NX + 2 * X0, NX + 2 * XF
def src_span(side, length, first, last):
    if side > 0:
        return pl.ds(length - last, last - first + 1)
    if side < 0:
        return pl.ds(first - 1, last - first + 1)
    return pl.ds(0, length)


def dst_span(side, length, own, first, last):
    if side > 0:
        return pl.ds(own - last, last - first + 1)
    if side < 0:
        return pl.ds(own + length + first - 1, last - first + 1)
    return pl.ds(own, length)


def planes(first, end, together, body):
    main = (end - first) // together * together

    if main > together:

        @pl.loop(first, first + main, step=together)
        def _(x):
            for j in range(together):
                body(x + j)

    else:
        main = 0
    for x in range(first + main, end):
        body(x)


def runs_of(sx, sy):
    runs = []
    for i, (cx, cy, _) in enumerate(VELOCITIES):
        depth = (2 - sx * cx, 2 - sy * cy)
        if runs and runs[-1][2] == depth:
            runs[-1] = (runs[-1][0], runs[-1][1] + 1, depth)
        else:
            runs.append((i, 1, depth))
    return runs


def rows_in(*parts):
    return sum(math.prod(p.shape) // NZ for p in parts)


def exchange_kernel(
    pop, vel, heat, obj, liq, span,
    state_out, sens, scale_out, gain_out,
    s0, s1, u0, obj0, liq0, span0, heat0, um, ka, kb, extras, count,
    load_sem, ssem, rsem, ready,
):
    grp, blk = lax.axis_index("grp"), lax.axis_index("blk")
    n_grp, n_blk = lax.axis_size("grp"), lax.axis_size("blk")
    def exists(d):
        ok = None
        for side, at, n in ((d[0], grp, n_grp), (d[1], blk, n_blk)):
            if side:
                one = at < n - 1 if side > 0 else at > 0
                ok = one if ok is None else ok & one
        return ok

    def origin(d):
        return (grp + d[0] == 0) & (blk + d[1] == 0)

    def mutual(d):
        return ~origin((0, 0)) & ~origin(d)

    def first(d):
        if d[1] > 0:
            later = ~origin((0, 0))
        elif d[1] < 0:
            later = origin(d)
        else:
            later = origin(d) | (~origin((0, 0)) & (grp % 2 == 1))
        return later & ~mutual(d)

    def ahead(d):
        return exists(d) & ~first(d)

    def opposite(d):
        return (-d[0], -d[1])

    def peer(d):
        return dict(device_id=(grp + d[0], blk + d[1]), device_id_type=MESH)

    def remote(d, j, src, dst):
        k = DIRS.index(d)
        to = peer((d[0], 0)) if j == PASSED else peer(d)
        return pltpu.make_async_remote_copy(
            src_ref=src, dst_ref=dst, send_sem=ssem.at[j, k], recv_sem=rsem.at[j, k], **to
        )

    def part(d, src, dst, lead, depth, own_x, cut=None, rows=None):
        xs, ys = src_span(d[0], NX, 1, depth[0]), src_span(d[1], NY, 1, depth[1])
        xd = dst_span(d[0], NX, own_x, 1, depth[0])
        yd = dst_span(d[1], NY, Y0, 1, depth[1])
        if cut:
            xs, xd = pl.ds(cut[0], cut[1]), pl.ds(own_x + cut[0], cut[1])
        if rows:
            ys, yd = pl.ds(rows[0], rows[1]), pl.ds(Y0 + rows[0], rows[1])
        return src.at[lead + (xs, ys)], dst.at[lead + (xd, yd)]

    def state_parts(d, *cuts):
        parts = [part(d, pop, s0, (pl.ds(a, n),), depth, X0, *cuts) for a, n, depth in runs_of(*d)]
        parts.append(part(d, vel, u0, (pl.ds(0, 3),), (2, 2), X0, *cuts))
        parts.append(part(d, obj, obj0, (), (2, 2), X0, *cuts))
        parts.append(part(d, liq, liq0, (), (2, 2), X0, *cuts))
        return parts

    even = grp % 2 == 0

    def rim_parts(d):
        if not d[0]:
            return state_parts(d, (jnp.where(even, 0, 3), NX - 3))
        return state_parts(d, None, None if d[1] else (0, LOW_ROWS))

    def upper_parts(d):
        return state_parts(d, None, (LOW_ROWS, NY - LOW_ROWS))

    def near_parts(d):
        return state_parts(d, (jnp.where(even, NX - 3, 0), 3))

    def passed_parts(d):
        dx, dy = d
        parts = []

        def add(frame, lead, depth):
            rows = dst_span(dy, NY, Y0, 1, depth[1])
            xs = src_span(dx, NX, 1, depth[0])
            xs, xd = pl.ds(X0 + xs.start, xs.size), dst_span(dx, NX, X0, 1, depth[0])
            parts.append((frame.at[lead + (xs, rows)], frame.at[lead + (xd, rows)]))

        for a, n, depth in runs_of(*d):
            add(s0, (pl.ds(a, n),), depth)
        add(u0, (pl.ds(0, 3),), (2, 2))
        add(obj0, (), (2, 2))
        add(liq0, (), (2, 2))
        return parts

    def direct(d):
        return (even if d[0] < 0 else ~even) if d[0] and d[1] else True

    def passes(d):
        return exists((0, -d[1])) & ~direct(d)

    def filter_pieces(d):
        dx, dy = d
        if dx and dy:
            near = ((1, 3, 1, 7), (4, 7, 1, 4))
        else:
            near = ((1, XF, 1, XF),)
        return [
            (src_span(dx, NX, a, b), src_span(dy, NY, c, e),
             dst_span(dx, NX, XF, a, b), dst_span(dy, NY, Y0, c, e))
            for a, b, c, e in near
        ]

    def span_parts(d):
        return [(span.at[xs, ys], span0.at[xd, yd]) for xs, ys, xd, yd in filter_pieces(d)]

    def sens_parts(d):
        pieces = filter_pieces(d)
        if not d[1]:
            xs, _, xd, _ = pieces[0]
            halves = (0, NY // 2), (NY // 2, NY // 2)
            pieces = [(xs, pl.ds(a, n), xd, pl.ds(Y0 + a, n)) for a, n in halves]
        return [
            (sens.at[pl.ds(xs.start + XF, xs.size), pl.ds(ys.start + Y0, ys.size)], sens.at[xd, yd])
            for xs, ys, xd, yd in pieces
        ]

    RIM, SPAN, SENS, NEAR, PASSED, UPPER = range(6)
    stages = (rim_parts, span_parts, sens_parts, near_parts, passed_parts, upper_parts)

    def whole(j, d):
        rows = count.at[pl.ds(0, rows_in(*(src for src, _ in stages[j](d))))]
        return remote(d, j, rows, rows)

    def send(j, d, half=0):
        parts = stages[j](d)
        if j == SENS and not d[1]:
            parts = parts[half : half + 1]
        for src, dst in parts:
            remote(d, j, src, dst).start()

    def sends(j, d):
        return passes(d) if j == PASSED else exists(d) & direct(d) if j == RIM else exists(d)

    def gets(j, d):
        if j == PASSED:
            return exists((0, -d[1])) & direct(d)
        if j == RIM and d[0] and d[1]:
            return exists(opposite(d)) & ~direct(d)
        return exists(opposite(d))

    def directions(j):
        if j == NEAR:
            return ((0, 1), (0, -1))
        if j == UPPER:
            return ((1, 0), (-1, 0))
        if j == PASSED:
            return ((1, 1), (1, -1), (-1, 1), (-1, -1))
        return DIRS

    def wait_recv(j):
        for d in directions(j):
            pl.when(gets(j, d))(lambda d=d: whole(j, d).wait_recv())

    def wait_send(j):
        for d in directions(j):
            pl.when(sends(j, d))(lambda d=d: whole(j, d).wait_send())

    barrier = pltpu.get_barrier_semaphore()
    expected = 0
    for d in DIRS:
        before = exists(d) & (first(d) | mutual(d))
        pl.when(before)(lambda d=d: pl.semaphore_signal(barrier, inc=1, **peer(d)))
        expected += jnp.where(ahead(d), 1, 0)
    pl.when(expected > 0)(lambda: pl.semaphore_wait(barrier, expected))

    corners = ((1, 1), (1, -1), (-1, 1), (-1, -1))
    order = corners + ((1, 0), (-1, 0), (0, 1), (0, -1))
    work = [(RIM, d) for d in ((1, 1), (-1, 1), (1, 0), (-1, 0))] + [(NEAR, (0, 1)), (NEAR, (0, -1))]
    work += [(UPPER, (1, 0)), (UPPER, (-1, 0)), (RIM, (1, -1)), (RIM, (-1, -1))]
    work += [(RIM, (0, 1)), (RIM, (0, -1))]

    def greet(d):
        pl.semaphore_signal(ready.at[DIRS.index(d)], inc=1, **peer(d))

    for d in order:
        pl.when(ahead(d) & ~mutual(d))(lambda d=d: greet(d))
    for j, d in work:
        pl.when(ahead(d) & sends(j, d))(lambda j=j, d=d: send(j, d))

    own = (pl.ds(X0, NX), pl.ds(Y0, NY))
    loads = [
        pltpu.make_async_copy(src, dst, load_sem.at[j])
        for j, (src, dst) in enumerate(
            (
                (pop, s0.at[(pl.ds(0, 19),) + own]),
                (vel, u0.at[(pl.ds(0, 3),) + own]),
                (obj, obj0.at[own]),
                (liq, liq0.at[own]),
                (heat, heat0),
                (span, span0.at[pl.ds(XF, NX), pl.ds(Y0, NY)]),
            )
        )
    ]
    for c in loads:
        c.start()

    for d in ((1, 0), (-1, 0), (1, 1), (-1, 1), (0, 1), (0, -1), (-1, -1)):

        @pl.when(exists(d) & first(d))
        def _():
            pl.semaphore_wait(ready.at[DIRS.index(opposite(d))], 1)
            for j, to in work:
                if to == d:
                    pl.when(sends(j, d))(lambda j=j, d=d: send(j, d))

    def outside(x_step, x_filter, rows):
        def fill(first, count, width, put):
            @pl.loop(first, first + count)
            def _(x):
                for r in rows:
                    put(x, pl.ds(r, 8))

        zero = jnp.zeros((8, NZ), jnp.float32)
        none = jnp.full((8, NZ), -1, jnp.int32)

        def put_step(x, r):
            for i in range(19):
                s0[i, x, r] = zero
            for i in range(3):
                u0[i, x, r] = zero
            obj0[x, r] = zero
            liq0[x, r] = none

        def put_filter(x, r):
            span0[x, r] = none
            sens[x, r] = zero

        fill(*x_step, None, put_step)
        fill(*x_filter, None, put_filter)

    groups = (8, 16, 24, 32)
    pl.when(grp == 0)(lambda: outside((0, X0), (0, XF), groups))
    pl.when(grp == n_grp - 1)(lambda: outside((X0 + NX, X0), (XF + NX, XF), groups))
    pl.when(blk == 0)(lambda: outside((0, STEP_X), (0, FILTER_X), (8,)))
    pl.when(blk == n_blk - 1)(lambda: outside((0, STEP_X), (0, FILTER_X), (32,)))

    wait_recv(NEAR)
    for d in corners:
        pl.when(passes(d))(lambda d=d: send(PASSED, d))
    for d in order:
        pl.when(exists(d))(lambda d=d: send(SPAN, d))
    for c in loads:
        c.wait()
    lane = lax.broadcasted_iota(jnp.int32, (8, NZ), 1)

    def step(number, src, x, r0):
        def pulled(i):
            cx, cy, cz = VELOCITIES[i]
            v = src[i, x + cx, pl.ds(r0 + cy, 8)]
            if cz > 0:
                return jnp.where(lane == NZ - 1, 0.0, pltpu.roll(v, NZ - 1, 1))
            if cz < 0:
                return jnp.where(lane == 0, 0.0, pltpu.roll(v, 1, 1))
            return v

        p = [pulled(i) for i in range(19)]
        rows = pl.ds(r0, 8)
        if number == 0:
            kind = liq0[x, rows]
            fluid = kind.astype(jnp.float32)
            inside = kind >= 0
            omega = 0.9 + 0.7 * fluid
            b = jnp.where(inside, omega, 0.0)
            a = jnp.where(inside, 1.0 - omega, 0.0)
            third = fluid * (3.0 / 36.0)
            ux, uy, uz = (u0[i, x, rows] * third for i in range(3))
            ka[x, rows] = a
            kb[x, rows] = b
            um[0, x, rows] = ux
            um[1, x, rows] = uy
            um[2, x, rows] = uz
        else:
            a, b = ka[x, rows], kb[x, rows]
            ux, uy, uz = (um[i, x, rows] for i in range(3))
        total = {i: p[i] + p[i + 1] for i in range(1, 19, 2)}
        diff = {i: p[i] - p[i + 1] for i in range(1, 19, 2)}
        faces = total[1] + total[3] + total[5]
        edges = (total[7] + total[9]) + (total[11] + total[13]) + (total[15] + total[17])
        average = p[0] * (1.0 / 3.0) + faces * (1.0 / 18.0) + edges * (1.0 / 36.0)
        mx = (diff[1] + diff[1]) + (diff[7] + diff[9]) + (diff[11] + diff[13])
        my = (diff[3] + diff[3]) + (diff[7] - diff[9]) + (diff[15] + diff[17])
        mz = (diff[5] + diff[5]) + (diff[11] - diff[13]) + (diff[15] - diff[17])
        extra = ux * mx + uy * my + uz * mz
        pushed = b * (average + extra)
        o = obj0[x, rows] * (1.0 / 36.0)
        o2 = o + o
        adds = (pushed + 12.0 * o, pushed + o2, pushed + o)
        return [a * p[i] + adds[0 if i == 0 else 1 if i < 7 else 2] for i in range(19)], extra

    def step_1(starts, x):
        for r0 in starts:
            rows = pl.ds(r0, 8)
            posts, extra = step(0, s0, x, r0)
            for i in range(19):
                s1[i, x, rows] = posts[i]
            extras[0, x, rows] = extra

    def step_2(starts, x):
        for r0 in starts:
            rows = pl.ds(r0, 8)
            posts, extra = step(1, s1, x, r0)
            for i in range(19):
                s0[i, x, rows] = posts[i]
            extras[1, x, rows] = extra

    def step_3(starts, x):
        for r0 in starts:
            rows, here = pl.ds(r0, 8), pl.ds(r0 - Y0, 8)
            posts, extra = step(2, s0, x, r0)
            for i in range(19):
                state_out[i, x - X0, here] = posts[i]
            total = extras[0, x, rows] + extras[1, x, rows] + extra
            sens[x - X0 + XF, rows] = heat0[x - X0, here] * total

    for side in (1, -1):
        low = side > 0
        starts = ((Y0 - 2, Y0 + 2), (Y0 - 1, Y0 + 1), (Y0,)) if low else ((Y0 + 10,), (Y0 + 9,), (Y0 + 8,))
        one, two, three = (functools.partial(f, r) for f, r in zip((step_1, step_2, step_3), starts))
        pl.when(gets(RIM, (0, side)))(lambda: whole(RIM, (0, side)).wait_recv())
        for d in corners:
            if d[1] == side:
                pl.when(sends(PASSED, d))(lambda d=d: whole(PASSED, d).wait_send())
        planes(X0 + 1, X0 + NX - 1, 3 if low else 6, one)
        planes(X0 + 2, X0 + NX - 2, 4, two)
        planes(X0 + 3, X0 + NX - 3, 2, three)
        for j in (RIM, PASSED, UPPER):
            for d in directions(j):
                if d[0] and (d[1] == side or (d[1] == 0 and low == (j == RIM))):
                    pl.when(gets(j, d))(lambda j=j, d=d: whole(j, d).wait_recv())
        for n, body in ((1, one), (2, two), (3, three)):
            planes(n, X0 + n, 3, body)
            planes(X0 + NX - n, STEP_X - n, 3, body)
        for d in order:
            if d[1] in (0, -side):
                pl.when(exists(d))(lambda d=d: send(SENS, d, 0 if low else 1))

    wait_recv(SPAN)

    def weigh(x):
        for r0 in groups:
            rows = pl.ds(r0, 8)
            k = span0[x, rows]
            r2 = jnp.where(k == 0, 0.25, jnp.where(k == 1, 1.0, jnp.where(k == 2, 4.0, 16.0)))
            gain = jnp.where(k >= 0, 1.0 / (1.0 + 6.0 * r2), 0.0)
            gain_out[x, rows] = gain
            scale_out[x, rows] = gain * r2

    planes(0, FILTER_X, 4, weigh)

    wait_recv(SENS)
    for j in (RIM, SPAN, SENS, NEAR, UPPER):
        wait_send(j)


def sweep_kernel(state, sens, scale, gain, state_out, smooth_out, own, q0, q1, smooth, sem):
    copies = (
        pltpu.make_async_copy(state, state_out, sem.at[0]),
        pltpu.make_async_copy(smooth, smooth_out, sem.at[1]),
    )
    copies[0].start()
    lane = lax.broadcasted_iota(jnp.int32, (8, NZ), 1)
    for number in range(1, SWEEPS + 1):
        last = number == SWEEPS
        src = sens if number == 1 else (q0 if number % 2 == 0 else q1)
        dst = q0 if number % 2 == 1 else q1
        reach = SWEEPS - number
        for x in range(number, FILTER_X - number):
            over = max(XF - x, x - XF - NX + 1, 0)
            low, high = Y0 - (reach - over), Y0 + NY + (reach - over)
            for r0 in list(range(low, high - 8, 8)) + [high - 8]:
                rows = pl.ds(r0, 8)
                mid = src[x, rows]
                beside = src[x - 1, rows] + src[x + 1, rows]
                beside += src[x, pl.ds(r0 - 1, 8)] + src[x, pl.ds(r0 + 1, 8)]
                beside += jnp.where(lane == NZ - 1, 0.0, pltpu.roll(mid, NZ - 1, 1))
                beside += jnp.where(lane == 0, 0.0, pltpu.roll(mid, 1, 1))
                if number == 1:
                    base = mid * gain[x, rows]
                    own[x, rows] = base
                else:
                    base = own[x, rows]
                value = base + scale[x, rows] * beside
                if last:
                    smooth[x - XF, pl.ds(r0 - Y0, 8)] = value
                else:
                    dst[x, rows] = value

    copies[1].start()
    for c in copies:
        c.wait()


def on_device(pop, vel, heat, obj, liq, span):
    f32, i32 = jnp.float32, jnp.int32
    vmem = pl.BlockSpec(memory_space=pltpu.VMEM)
    anywhere = pl.BlockSpec(memory_space=pltpu.HBM)
    frame = (FILTER_X, ROWS, NZ)
    step_frame = (STEP_X, ROWS, NZ)
    args = [
        pltpu.with_memory_space_constraint(x, pltpu.HBM)
        for x in (pop, vel, heat, obj, liq, span)
    ]
    state, sens, scale, gain = pl.pallas_call(
        exchange_kernel,
        out_shape=(
            jax.ShapeDtypeStruct((19, NX, NY, NZ), f32),
            jax.ShapeDtypeStruct(frame, f32),
            jax.ShapeDtypeStruct(frame, f32),
            jax.ShapeDtypeStruct(frame, f32),
        ),
        in_specs=[anywhere] * 6,
        out_specs=(vmem,) * 4,
        scratch_shapes=[
            pltpu.VMEM((19,) + step_frame, f32),
            pltpu.VMEM((19,) + step_frame, f32),
            pltpu.VMEM((3,) + step_frame, f32),
            pltpu.VMEM(step_frame, f32),
            pltpu.VMEM(step_frame, i32),
            pltpu.VMEM(frame, i32),
            pltpu.VMEM((NX, NY, NZ), f32),
            pltpu.VMEM((3,) + step_frame, f32),
            pltpu.VMEM(step_frame, f32),
            pltpu.VMEM(step_frame, f32),
            pltpu.VMEM((2,) + step_frame, f32),
            pltpu.VMEM((1024, NZ), f32),
            pltpu.SemaphoreType.DMA((6,)),
            pltpu.SemaphoreType.DMA((6, 8)),
            pltpu.SemaphoreType.DMA((6, 8)),
            pltpu.SemaphoreType.REGULAR((8,)),
        ],
        compiler_params=pltpu.CompilerParams(
            collective_id=0, has_side_effects=True, vmem_limit_bytes=36 << 20
        ),
        name="steps",
    )(*args)
    return pl.pallas_call(
        sweep_kernel,
        out_shape=(
            jax.ShapeDtypeStruct((19, NX, NY, NZ), f32),
            jax.ShapeDtypeStruct((NX, NY, NZ), f32),
        ),
        in_specs=[vmem] * 4,
        out_specs=(anywhere, anywhere),
        scratch_shapes=[
            pltpu.VMEM(frame, f32),
            pltpu.VMEM(frame, f32),
            pltpu.VMEM(frame, f32),
            pltpu.VMEM((NX, NY, NZ), f32),
            pltpu.SemaphoreType.DMA((2,)),
        ],
        compiler_params=pltpu.CompilerParams(vmem_limit_bytes=36 << 20),
        name="sweeps",
    )(state, sens, scale, gain)


def solution(mesh):
    field = P("grp", "blk", None)
    many = P(None, "grp", "blk", None)
    return jax.shard_map(
        on_device,
        mesh=mesh,
        in_specs=(many, many, field, field, field, field),
        out_specs=(many, field),
        check_vma=False,
    )
```
